32 devices in a mesh: beads: 8 (over y, x, core), waves: 4 (over z).
Axes of the slice: x: 2, y: 2, z: 4, core: 2. Of those that a mesh axis runs over, the one named last changes fastest.
Arguments:
- positions: float32 [3, 4096], P(None, 'beads'), may hold values from 0 to 256
- features: bfloat16 [4096, 256], P(('beads', 'waves')), may hold values from -6 to 6
- cotangent: bfloat16 [4096, 256], P(('beads', 'waves')), may hold values from -6 to 6
- wavevectors: float32 [3, 4096], replicated, may hold values from -0.25 to 0.25
- filter_gain: bfloat16 [4096, 256], P(('beads', 'waves')), may hold values from -6 to 6
Outputs:
- grad_features: bfloat16 [4096, 256], P(('beads', 'waves'))
- grad_positions: float32 [3, 4096], P(None, ('beads', 'waves'))
- grad_filter: float32 [4096, 256], P(('beads', 'waves'))
The draws below stay inside these ranges and needn't reach their ends.
All inputs are finite; a program needn't handle non-finite values.
Results may differ from the reference program's by a relative error of at most 0.012.
Values may be sent and summed in bfloat16 or wider, within the bound.
A program may use at most 64 MiB of HBM per device.

```python
import math
import jax
import jax.numpy as jnp
from jax import lax

WIDTH = 256
K = 4096
BEADS = 4096


def block_levels(own_key, dims, split, least, top_value):
    loudness, own = 1.0, jax.random.fold_in(own_key, 6)
    for dim, shards_of in split:
        heights = jnp.exp(jax.random.uniform(jax.random.fold_in(own, dim), (shards_of,), jnp.float32, least / len(split), top_value / len(split)))
        loudness = loudness * jnp.repeat(heights, dims[dim] // shards_of).reshape([-1 if axis == dim else 1 for axis in range(len(dims))])
    return loudness


def centred(own_key, shape, scale, limit, shards=(), held_as=jnp.bfloat16):
    entries = scale * jax.random.normal(own_key, shape, jnp.float32)
    if shards:
        entries = entries * block_levels(own_key, shape, shards, -0.22, 0.18)
    return jnp.clip(entries, -limit, limit).astype(held_as)


def setup_inputs(seed: int = 0) -> dict:
    streams_of = jax.random.split(jax.random.key(seed), 6)
    return {
        "positions": jnp.clip(256.0 * jax.random.uniform(streams_of[0], (3, BEADS), jnp.float32) ** block_levels(streams_of[0], (3, BEADS), ((1, 8),), -0.2, 0.2), 0.0, 256.0),
        "features": centred(streams_of[1], (BEADS, WIDTH), 1.0, 6.0, ((0, 32),)),
        "cotangent": centred(streams_of[2], (BEADS, WIDTH), 1.0, 6.0, ((0, 32),)),
        "wavevectors": jnp.clip(jax.random.uniform(streams_of[3], (3, K), jnp.float32, -0.25, 0.25), -0.25, 0.25),
        "filter_gain": centred(streams_of[4], (K, WIDTH), 1.0, 6.0, ((0, 32),)),
    }


def phases(pos, kvec):
    return pos[0][:, None] * kvec[0][None, :] + pos[1][:, None] * kvec[1][None, :] + pos[2][:, None] * kvec[2][None, :]

def reference(positions, features, cotangent, wavevectors, filter_gain):
    nbeads = features.shape[0]
    nwaves = wavevectors.shape[1]
    width = features.shape[1]
    blk = min(1024, nbeads)
    nblk = nbeads // blk
    spec_scale = 1.0 / math.sqrt(nbeads)
    wave_scale = 1.0 / math.sqrt(nwaves)
    pos_blocks = positions.reshape(3, nblk, blk).transpose(1, 0, 2)
    feat_blocks = features.reshape(nblk, blk, width)
    cot_blocks = cotangent.reshape(nblk, blk, width)

    def accumulate(total, items):
        pos, feat, cot = items
        theta = phases(pos, wavevectors)
        cosine = jnp.cos(theta).astype(jnp.bfloat16).astype(jnp.float32)
        sine = jnp.sin(theta).astype(jnp.bfloat16).astype(jnp.float32)
        joined = jnp.concatenate([feat, cot], 1).astype(jnp.float32)
        part_cos = jnp.dot(cosine.T, joined)
        part_sin = jnp.dot(sine.T, joined)
        term = jnp.concatenate([part_cos[:, :width] * spec_scale, part_sin[:, :width] * spec_scale, part_cos[:, width:] * wave_scale, part_sin[:, width:] * wave_scale], 1)
        return (total + term, None)
    start = jnp.zeros((nwaves, 4 * width), jnp.float32)
    total, _ = lax.scan(accumulate, start, (pos_blocks, feat_blocks, cot_blocks))
    spec_r = total[:, :width]
    spec_i = total[:, width:2 * width]
    cot_r = total[:, 2 * width:3 * width]
    cot_i = total[:, 3 * width:]
    gains = filter_gain.astype(jnp.float32)
    grad_filter = cot_r * spec_r + cot_i * spec_i
    filt_r = (gains * spec_r).astype(jnp.bfloat16).astype(jnp.float32)
    filt_i = (gains * spec_i).astype(jnp.bfloat16).astype(jnp.float32)
    dspec_r = (gains * cot_r).astype(jnp.bfloat16).astype(jnp.float32)
    dspec_i = (gains * cot_i).astype(jnp.bfloat16).astype(jnp.float32)

    def backward(items):
        pos, feat, cot = items
        theta = phases(pos, wavevectors)
        cosine = jnp.cos(theta).astype(jnp.bfloat16).astype(jnp.float32)
        sine = jnp.sin(theta).astype(jnp.bfloat16).astype(jnp.float32)
        feat32 = feat.astype(jnp.float32)
        cot32 = cot.astype(jnp.float32)
        grad_feat = (jnp.dot(cosine, dspec_r) + jnp.dot(sine, dspec_i)) * spec_scale
        first = jnp.dot(cot32, filt_r.T) * wave_scale + jnp.dot(feat32, dspec_r.T) * spec_scale
        second = jnp.dot(cot32, filt_i.T) * wave_scale + jnp.dot(feat32, dspec_i.T) * spec_scale
        dtheta = -sine * first + cosine * second
        grad_pos = jnp.dot(wavevectors, dtheta.T, precision=lax.Precision.HIGHEST)
        return (grad_feat, grad_pos)
    grad_feat, grad_pos = lax.map(backward, (pos_blocks, feat_blocks, cot_blocks))
    grad_features = grad_feat.reshape(nbeads, width).astype(jnp.bfloat16)
    grad_positions = grad_pos.transpose(1, 0, 2).reshape(3, nbeads)
    return (grad_features, grad_positions, grad_filter)
```

```python
import functools
import math

import jax
import jax.numpy as jnp
from jax import lax
from jax.experimental import pallas as pl
from jax.experimental.pallas import tpu as pltpu
from jax.sharding import PartitionSpec as P

MESH = pl.DeviceIdType.MESH
PLANE = 4
LANES = 128


def flip(i, q):
    out = i
    if q % 2:
        out = out + 1 - 2 * (i % 2)
    if q // 2:
        out = out + 2 - 4 * ((i // 2) % 2)
    return out


def sincos(theta):
    n = jnp.round(theta * (2.0 / math.pi))
    k = n.astype(jnp.int32)
    r = (theta - n * 1.5703125) - n * 4.83826794896619e-4
    r2 = r * r
    s = r + r * r2 * (-1.6666654611e-1 + r2 * (8.3321608736e-3 - r2 * 1.9515295891e-4))
    c = (1.0 - 0.5 * r2) + r2 * r2 * (
        4.166664568298827e-2 + r2 * (-1.388731625493765e-3 + r2 * 2.443315711809948e-5)
    )
    swap = (k & 1) == 1
    sv = jnp.where(swap, c, s)
    cv = jnp.where(swap, s, c)
    sv = jnp.where((k & 2) == 2, -sv, sv)
    cv = jnp.where(((k + 1) & 2) == 2, -cv, cv)
    return cv, sv


def kernel(
    nz, spec_scale, wave_scale,
    pos_ref, feat_ref, cot_ref, kvec_ref, gain_ref,
    gfeat_ref, gpos_ref, gfilt_ref,
    pos_all, joined, kcol, cs, acc, mid_tx, mid_rx, ebuf, dt, pf, sb, rx, rz,
    send_sem, recv_sem,
):
    own = feat_ref.shape[0]
    width = feat_ref.shape[1]
    per = gain_ref.shape[0]
    block = nz * own
    kk = 2 * per
    b = lax.axis_index("beads")
    z = lax.axis_index("waves")
    core = b % 2
    plane = b // 2
    partner = (b + 1 - 2 * core, z)
    near = [None] + [(flip(plane, r) * 2 + core, z) for r in range(1, PLANE)]
    far = [None] + [(b, flip(z, q)) for q in range(1, nz)]
    zq = [flip(z, q) for q in range(nz)]
    peers = [partner] + near[1:] + far[1:]

    barrier = pltpu.get_barrier_semaphore()
    for peer in peers:
        pl.semaphore_signal(barrier, inc=1, device_id=peer, device_id_type=MESH)

    ids = {}
    pending = []

    def copy(name, src, dst, to):
        i = ids.setdefault(name, len(ids))
        return pltpu.make_async_remote_copy(
            src_ref=src, dst_ref=dst, send_sem=send_sem.at[i], recv_sem=recv_sem.at[i],
            device_id=to, device_id_type=MESH,
        )

    def send(name, src, dst, to):
        c = copy(name, src, dst, to)
        c.start()
        pending.append(c)
        return c

    def rows(q):
        return pl.ds(pl.multiple_of(zq[q] * own, own), own)

    pos_all[0] = pos_ref[...]
    joined[0, rows(0), :width] = feat_ref[...]
    joined[0, rows(0), width:] = cot_ref[...]
    pl.semaphore_wait(barrier, len(peers))

    got = {}
    for r in range(1, PLANE):
        got["p", r] = send(("p", r), pos_all.at[0], pos_all.at[r], near[r])

    def hop(r, q, src, to):
        got[r, q] = send((r, q), joined.at[src, rows(q)], joined.at[r, rows(q)], to)

    hop(1, 0, 0, near[1])
    hop(2, 0, 0, near[2])
    for q in range(1, nz):
        got[0, q] = send((0, q), joined.at[0, rows(0)], joined.at[0, rows(0)], far[q])

    eye = lax.broadcasted_iota(jnp.int32, (per, per), 0) == lax.broadcasted_iota(
        jnp.int32, (per, per), 1
    )
    for g in range(2):
        owner = (b + g * (1 - 2 * core)) * nz + z
        piece = kvec_ref[:, pl.ds(pl.multiple_of(owner * per, per), per)]
        for d in range(3):
            line = jnp.where(eye, jnp.broadcast_to(piece[d : d + 1], (per, per)), 0.0)
            kcol[d, g * per : (g + 1) * per, :] = jnp.broadcast_to(
                jnp.sum(line, axis=1, keepdims=True), (per, LANES)
            )

    step = 16
    per_group = per // step
    wide = block // LANES

    def waves(r):
        p = pos_all[r]

        def one(i, _):
            at = pl.ds(pl.multiple_of(i * step, step), step)
            k0, k1, k2 = (jnp.concatenate([kcol[d, at, :]] * wide, 1) for d in range(3))
            theta = p[0:1] * k0 + p[1:2] * k1 + p[2:3] * k2
            cv, sv = sincos(theta)
            base = (i // per_group) * kk + (i % per_group) * step
            cs[r, pl.ds(pl.multiple_of(base, step), step), :] = cv.astype(jnp.bfloat16)
            cs[r, pl.ds(pl.multiple_of(base + per, step), step), :] = sv.astype(jnp.bfloat16)
            return 0

        lax.fori_loop(0, 2 * per_group, one, 0)

    def spread(r, first):
        term = jnp.dot(cs[r], joined[r], preferred_element_type=jnp.float32)
        if first:
            acc[...] = term
        else:
            acc[...] += term

    def arrive(r, q):
        got[r, q].wait_recv()

    half = nz // 2
    waves(0)
    arrive(2, 0)
    hop(3, 0, 2, near[1])
    for q in range(1, nz):
        arrive(0, q)
        hop(1, q, 0, near[1])
        hop(2, q, 0, near[2])
        if q == 1:
            spread_ready = True
        arrive(1, q - 1)
        if q >= 2:
            arrive(2, q - 1)
        if q < half:
            pass
        if q - 1 >= half:
            hop(3, q - 1, 1, near[2])
        elif q - 1 > 0:
            hop(3, q - 1, 2, near[1])
        if q < PLANE:
            got["p", q].wait_recv()
            waves(q)
    spread(0, True)
    arrive(1, nz - 1)
    arrive(2, nz - 1)
    hop(3, nz - 1, 1, near[2])
    spread(1, False)
    spread(2, False)
    for q in range(nz):
        arrive(3, q)
    spread(3, False)

    mid_tx[...] = acc[kk:, :].astype(jnp.bfloat16)
    first = send("m1", mid_tx, mid_rx, partner)
    first.wait_recv()
    total = acc[:kk, :] + mid_rx[...].astype(jnp.float32)
    gain = gain_ref[...].astype(jnp.float32)
    sr, gr = total[:per, :width] * spec_scale, total[:per, width:] * wave_scale
    si, gi = total[per:, :width] * spec_scale, total[per:, width:] * wave_scale
    gfilt_ref[...] = gr * sr + gi * si
    ebuf[:per, :width] = (gain * gr * spec_scale).astype(jnp.bfloat16)
    ebuf[:per, width:] = (gain * sr * wave_scale).astype(jnp.bfloat16)
    ebuf[per:kk, :width] = (gain * gi * spec_scale).astype(jnp.bfloat16)
    ebuf[per:kk, width:] = (gain * si * wave_scale).astype(jnp.bfloat16)
    second = send("m2", ebuf.at[:kk], ebuf.at[kk:], partner)
    second.wait_recv()
    dt[...] = jnp.transpose(ebuf[:, :width].astype(jnp.float32)).astype(jnp.bfloat16)

    tall = pf.shape[2]
    cols = 2 * own
    halves = block // cols

    def fold(r):
        def one(h, _):
            at = pl.ds(pl.multiple_of(h * cols, cols), cols)
            trig = cs[r, :, at]
            grad = jnp.dot(dt[...], trig, preferred_element_type=jnp.float32)
            ab = lax.dot_general(
                ebuf[...], joined[r, at, :], (((1,), (1,)), ((), ())),
                preferred_element_type=jnp.float32,
            )
            sums = [jnp.zeros((1, cols), jnp.float32)] * 3
            for g in range(2):
                lo = g * kk
                dth = (
                    trig[lo : lo + per].astype(jnp.float32) * ab[lo + per : lo + kk]
                    - trig[lo + per : lo + kk].astype(jnp.float32) * ab[lo : lo + per]
                )
                for d in range(3):
                    k = jnp.concatenate([kcol[d, g * per : (g + 1) * per, :]] * (cols // LANES), 1)
                    sums[d] = sums[d] + jnp.sum(dth * k, axis=0, keepdims=True)
            rest = jnp.zeros((tall - width - 3, cols), jnp.float32)
            tail = jnp.concatenate(sums + [rest], 0)
            for j in range(2):
                lane = slice(j * own, (j + 1) * own)
                pf[r, h * 2 + j, :width, :] = grad[:, lane]
                pf[r, h * 2 + j, width:, :] = tail[:, lane]
            return 0

        lax.fori_loop(0, halves, one, 0)

    def give(r, q, to, dst, *extra):
        value = pf[r, zq[q]]
        for e in extra:
            value = value + e[...].astype(jnp.float32)
        sb[r, q] = value.astype(jnp.bfloat16)
        got["g", r, q] = send(("g", r, q), sb.at[r, q], dst, to)

    fold(3)
    for q in reversed(range(nz)):
        give(3, q, near[1] if q < half else near[2], rx.at[2, q])
    fold(1)
    fold(2)
    for q in reversed(range(nz)):
        if q >= half:
            give(2, q, near[2], rx.at[1, q])
            got["g", 3, q].wait_recv()
            give(1, q, near[1], rx.at[0, q], rx.at[2, q])
        else:
            give(1, q, near[1], rx.at[0, q])
            got["g", 3, q].wait_recv()
            give(2, q, near[2], rx.at[1, q], rx.at[2, q])
    fold(0)
    for q in reversed(range(1, nz)):
        got["g", 1, q].wait_recv()
        got["g", 2, q].wait_recv()
        give(0, q, far[q], rz.at[q], rx.at[0, q], rx.at[1, q])
    got["g", 1, 0].wait_recv()
    got["g", 2, 0].wait_recv()
    out = pf[0, zq[0]] + rx[0, 0].astype(jnp.float32) + rx[1, 0].astype(jnp.float32)
    for q in reversed(range(1, nz)):
        got["g", 0, q].wait_recv()
        out = out + rz[q].astype(jnp.float32)
    gfeat_ref[...] = jnp.transpose(out[:width]).astype(jnp.bfloat16)
    gpos_ref[...] = out[width : width + 3]
    for c in pending:
        c.wait_send()


def fused(nz, beads_all, positions, features, cotangent, wavevectors, filter_gain):
    own, width = features.shape
    per = filter_gain.shape[0]
    block = nz * own
    tall = width + 16
    copies = 3 + PLANE * nz + 2 + PLANE * nz
    spec_scale = 1.0 / math.sqrt(beads_all)
    wave_scale = 1.0 / math.sqrt(wavevectors.shape[1])
    bf, f32 = jnp.bfloat16, jnp.float32
    vmem = pl.BlockSpec(memory_space=pltpu.VMEM)
    return pl.pallas_call(
        functools.partial(kernel, nz, spec_scale, wave_scale),
        out_shape=(
            jax.ShapeDtypeStruct((own, width), bf),
            jax.ShapeDtypeStruct((3, own), f32),
            jax.ShapeDtypeStruct((per, width), f32),
        ),
        in_specs=[vmem] * 5,
        out_specs=(vmem,) * 3,
        scratch_shapes=[
            pltpu.VMEM((PLANE, 3, block), f32),
            pltpu.VMEM((PLANE, block, 2 * width), bf),
            pltpu.VMEM((3, 2 * per, LANES), f32),
            pltpu.VMEM((PLANE, 4 * per, block), bf),
            pltpu.VMEM((4 * per, 2 * width), f32),
            pltpu.VMEM((2 * per, 2 * width), bf),
            pltpu.VMEM((2 * per, 2 * width), bf),
            pltpu.VMEM((4 * per, 2 * width), bf),
            pltpu.VMEM((width, 4 * per), bf),
            pltpu.VMEM((PLANE, nz, tall, own), f32),
            pltpu.VMEM((PLANE, nz, tall, own), bf),
            pltpu.VMEM((3, nz, tall, own), bf),
            pltpu.VMEM((nz, tall, own), bf),
            pltpu.SemaphoreType.DMA((copies,)),
            pltpu.SemaphoreType.DMA((copies,)),
        ],
        compiler_params=pltpu.CompilerParams(
            collective_id=0, has_side_effects=True, vmem_limit_bytes=40 << 20
        ),
    )(positions, features, cotangent, wavevectors, filter_gain)


def phases(pos, kvec):
    return (
        pos[0][:, None] * kvec[0][None, :]
        + pos[1][:, None] * kvec[1][None, :]
        + pos[2][:, None] * kvec[2][None, :]
    )


def contract_rows(left, right):
    return lax.dot_general(
        left, right, (((1,), (1,)), ((), ())), preferred_element_type=jnp.float32
    )


def contract_cols(left, right):
    return lax.dot_general(
        left, right, (((0,), (0,)), ((), ())), preferred_element_type=jnp.float32
    )


def filtered_spectra(term, gains, width):
    spec_r = term[:, :width]
    spec_i = term[:, width : 2 * width]
    cot_r = term[:, 2 * width : 3 * width]
    cot_i = term[:, 3 * width :]
    grad_filter = cot_r * spec_r + cot_i * spec_i
    stacked = jnp.concatenate(
        [gains * spec_r, gains * spec_i, gains * cot_r, gains * cot_i], 1
    ).astype(jnp.bfloat16)
    return (stacked, grad_filter)


def body(positions, features, cotangent, wavevectors, filter_gain):
    n_beads = lax.axis_size("beads")
    n_waves = lax.axis_size("waves")
    feats, cots = (
        lax.all_gather(features, "waves", axis=0, tiled=True),
        lax.all_gather(cotangent, "waves", axis=0, tiled=True),
    )
    beads_dev = feats.shape[0]
    width = feats.shape[1]
    waves_all = wavevectors.shape[1]
    per_owner = waves_all // (n_beads * n_waves)
    waves_dev = per_owner * n_beads
    spec_scale = 1.0 / math.sqrt(beads_dev * n_beads)
    wave_scale = 1.0 / math.sqrt(waves_all)
    grid = wavevectors.reshape(3, n_beads, n_waves, per_owner)
    local_waves = lax.dynamic_slice_in_dim(grid, lax.axis_index("waves"), 1, 2).reshape(
        3, waves_dev
    )
    joined = jnp.concatenate([feats, cots], 1)
    block = min(512, waves_dev)
    turns = waves_dev // block

    def fold_step(carry, piece, start):
        grad_feat, grad_pos = carry
        count = piece.shape[0]
        kvec = lax.dynamic_slice_in_dim(local_waves, start, count, 1)
        theta = phases(positions, kvec)
        cosine = jnp.cos(theta).astype(jnp.bfloat16)
        sine = jnp.sin(theta).astype(jnp.bfloat16)
        filt_r = piece[:, :width]
        filt_i = piece[:, width : 2 * width]
        dspec_r = piece[:, 2 * width : 3 * width]
        dspec_i = piece[:, 3 * width :]
        feat_term = (
            jnp.dot(cosine, dspec_r, preferred_element_type=jnp.float32)
            + jnp.dot(sine, dspec_i, preferred_element_type=jnp.float32)
        ) * spec_scale
        first = (
            contract_rows(cots, filt_r) * wave_scale + contract_rows(feats, dspec_r) * spec_scale
        )
        second = (
            contract_rows(cots, filt_i) * wave_scale + contract_rows(feats, dspec_i) * spec_scale
        )
        dtheta = -sine.astype(jnp.float32) * first + cosine.astype(jnp.float32) * second
        pos_term = lax.dot_general(
            kvec,
            dtheta,
            (((1,), (1,)), ((), ())),
            precision=lax.Precision.HIGHEST,
            preferred_element_type=jnp.float32,
        )
        return (grad_feat + feat_term, grad_pos + pos_term)

    kvec = local_waves
    theta = phases(positions, kvec)
    cosine = jnp.cos(theta).astype(jnp.bfloat16)
    sine = jnp.sin(theta).astype(jnp.bfloat16)
    part_cos = contract_cols(cosine, joined)
    part_sin = contract_cols(sine, joined)
    term = lax.psum_scatter(
        jnp.concatenate(
            [
                part_cos[:, :width] * spec_scale,
                part_sin[:, :width] * spec_scale,
                part_cos[:, width:] * wave_scale,
                part_sin[:, width:] * wave_scale,
            ],
            1,
        ),
        "beads",
        scatter_dimension=0,
        tiled=True,
    )
    owned, grad_filter = filtered_spectra(term, filter_gain.astype(jnp.float32), width)
    stacked = lax.all_gather(owned, "beads", axis=0, tiled=True)

    def sweep(step, carry):
        piece = lax.dynamic_slice_in_dim(stacked, step * block, block, 0)
        return fold_step(carry, piece, step * block)

    initial = (jnp.zeros((beads_dev, width), jnp.float32), jnp.zeros((3, beads_dev), jnp.float32))
    grads = lax.fori_loop(0, turns, sweep, initial)
    grad_feat, grad_pos = (
        lax.psum_scatter(
            grads[0].astype(jnp.bfloat16), "waves", scatter_dimension=0, tiled=True
        ).astype(jnp.float32),
        lax.psum_scatter(
            grads[1].astype(jnp.bfloat16), "waves", scatter_dimension=1, tiled=True
        ).astype(jnp.float32),
    )
    return (grad_feat.astype(jnp.bfloat16), grad_pos, grad_filter)


def suits(mesh):
    return mesh.shape["beads"] == 2 * PLANE and mesh.shape["waves"] == PLANE


def solution(mesh):
    placed = (
        P(None, "beads"),
        P(("beads", "waves"), None),
        P(("beads", "waves"), None),
        P(),
        P(("beads", "waves"), None),
    )

    def run(positions, features, *rest):
        part = body
        if suits(mesh):
            part = functools.partial(fused, mesh.shape["waves"], features.shape[0])
        return jax.shard_map(
            part,
            mesh=mesh,
            in_specs=placed,
            out_specs=(
                P(("beads", "waves"), None),
                P(None, ("beads", "waves")),
                P(("beads", "waves"), None),
            ),
            check_vma=False,
        )(positions, features, *rest)

    return run
```

```python
import functools
import math

import jax
import jax.numpy as jnp
from jax import lax
from jax.experimental import pallas as pl
from jax.experimental.pallas import tpu as pltpu
from jax.sharding import PartitionSpec as P

MESH = pl.DeviceIdType.MESH
PLANE = 4
LANES = 128


def flip(i, q):
    out = i
    if q % 2:
        out = out + 1 - 2 * (i % 2)
    if q // 2:
        out = out + 2 - 4 * ((i // 2) % 2)
    return out


def sincos(theta):
    n = jnp.round(theta * (2.0 / math.pi))
    k = n.astype(jnp.int32)
    r = (theta - n * 1.5703125) - n * 4.83826794896619e-4
    r2 = r * r
    s = r + r * r2 * (-1.6666654611e-1 + r2 * (8.3321608736e-3 - r2 * 1.9515295891e-4))
    c = (1.0 - 0.5 * r2) + r2 * r2 * (
        4.166664568298827e-2 + r2 * (-1.388731625493765e-3 + r2 * 2.443315711809948e-5)
    )
    swap = (k & 1) == 1
    sv = jnp.where(swap, c, s)
    cv = jnp.where(swap, s, c)
    sv = jnp.where((k & 2) == 2, -sv, sv)
    cv = jnp.where(((k + 1) & 2) == 2, -cv, cv)
    return cv, sv


def kernel(
    nz, spec_scale, wave_scale,
    pos_ref, feat_ref, cot_ref, kvec_ref, gain_ref,
    gfeat_ref, gpos_ref, gfilt_ref,
    pos_all, joined, kcol, cs, acc, mid_tx, mid_rx, ebuf, dt, pf, sb, rx, rz,
    send_sem, recv_sem, local_sem, kvecs, gains,
):
    own = feat_ref.shape[0]
    width = feat_ref.shape[1]
    per = gain_ref.shape[0]
    block = nz * own
    kk = 2 * per
    b = lax.axis_index("beads")
    z = lax.axis_index("waves")
    core = b % 2
    plane = b // 2
    partner = (b + 1 - 2 * core, z)
    near = [None] + [(flip(plane, r) * 2 + core, z) for r in range(1, PLANE)]
    far = [None] + [(b, flip(z, q)) for q in range(1, nz)]
    zq = [flip(z, q) for q in range(nz)]
    peers = [partner] + near[1:] + far[1:]

    barrier = pltpu.get_barrier_semaphore()
    for peer in peers:
        pl.semaphore_signal(barrier, inc=1, device_id=peer, device_id_type=MESH)

    ids = {}
    pending = []

    def copy(name, src, dst, to):
        i = ids.setdefault(name, len(ids))
        return pltpu.make_async_remote_copy(
            src_ref=src, dst_ref=dst, send_sem=send_sem.at[i], recv_sem=recv_sem.at[i],
            device_id=to, device_id_type=MESH,
        )

    def send(name, src, dst, to):
        c = copy(name, src, dst, to)
        c.start()
        pending.append(c)
        return c

    def rows(q):
        return pl.ds(pl.multiple_of(zq[q] * own, own), own)

    def part(q, j):
        return pl.ds(pl.multiple_of(zq[q] * own + j * (own // 2), own // 2), own // 2)

    loads = [
        pltpu.make_async_copy(src, dst, local_sem.at[i])
        for i, (src, dst) in enumerate(
            [
                (pos_ref, pos_all.at[0]),
                (feat_ref, joined.at[0, rows(0), :width]),
                (cot_ref, joined.at[0, rows(0), width:]),
                (kvec_ref, kvecs),
                (gain_ref, gains),
            ]
        )
    ]
    for c in loads:
        c.start()
    pl.semaphore_wait(barrier, len(peers))
    for c in loads[:3]:
        c.wait()

    got = {}
    for r in range(1, PLANE):
        got["p", r] = send(("p", r), pos_all.at[0], pos_all.at[r], near[r])

    def hop(r, q, src, to):
        got[r, q] = send((r, q), joined.at[src, rows(q)], joined.at[r, rows(q)], to)

    hop(1, 0, 0, near[1])
    hop(2, 0, 0, near[2])
    got[0, 1] = send((0, 1), joined.at[0, rows(0)], joined.at[0, rows(0)], far[1])

    loads[3].wait()
    eye = lax.broadcasted_iota(jnp.int32, (per, per), 0) == lax.broadcasted_iota(
        jnp.int32, (per, per), 1
    )
    for g in range(2):
        owner = (b + g * (1 - 2 * core)) * nz + z
        piece = kvecs[:, pl.ds(pl.multiple_of(owner * per, per), per)]
        for d in range(3):
            line = jnp.where(eye, jnp.broadcast_to(piece[d : d + 1], (per, per)), 0.0)
            kcol[d, g * per : (g + 1) * per, :] = jnp.broadcast_to(
                jnp.sum(line, axis=1, keepdims=True), (per, LANES)
            )

    step = 16
    per_group = per // step
    wide = block // LANES

    def waves(r):
        p = pos_all[r]

        def one(i, _):
            at = pl.ds(pl.multiple_of(i * step, step), step)
            k0, k1, k2 = (jnp.concatenate([kcol[d, at, :]] * wide, 1) for d in range(3))
            theta = p[0:1] * k0 + p[1:2] * k1 + p[2:3] * k2
            cv, sv = sincos(theta)
            base = (i // per_group) * kk + (i % per_group) * step
            cs[r, pl.ds(pl.multiple_of(base, step), step), :] = cv.astype(jnp.bfloat16)
            cs[r, pl.ds(pl.multiple_of(base + per, step), step), :] = sv.astype(jnp.bfloat16)
            return 0

        lax.fori_loop(0, 2 * per_group, one, 0)

    def spread(r, first):
        term = jnp.dot(cs[r], joined[r], preferred_element_type=jnp.float32)
        if first:
            acc[...] = term
        else:
            acc[...] += term

    def arrive(r, q):
        got[r, q].wait_recv()

    half = nz // 2

    def post(q):
        got[0, q] = send((0, q), joined.at[0, rows(0)], joined.at[0, rows(0)], far[q])

    post(2)
    post(3)
    waves(0)
    arrive(2, 0)
    hop(3, 0, 2, near[1])
    arrive(0, 1)
    hop(1, 1, 0, near[1])
    hop(2, 1, 0, near[2])
    got["p", 1].wait_recv()
    waves(1)
    arrive(0, 2)
    hop(1, 2, 0, near[1])
    hop(2, 2, 0, near[2])
    arrive(3, 0)
    got[3, 1] = send((3, 1), joined.at[3, rows(0)], joined.at[3, rows(0)], far[1])
    got["p", 2].wait_recv()
    waves(2)
    arrive(0, 3)
    hop(1, 3, 0, near[1])
    hop(2, 3, 0, near[2])
    spread(0, True)
    arrive(1, 2)
    hop(3, 2, 1, near[2])
    got["p", 3].wait_recv()
    waves(3)
    arrive(1, 3)
    got[3, 3] = send((3, 3), joined.at[1, part(3, 0)], joined.at[3, part(3, 0)], near[2])
    arrive(2, 3)
    got[3, 4] = send((3, 4), joined.at[2, part(3, 1)], joined.at[3, part(3, 1)], near[1])
    arrive(1, 0)
    arrive(1, 1)
    spread(1, False)
    arrive(2, 1)
    arrive(2, 2)
    spread(2, False)
    for q in range(1, 5):
        arrive(3, q)
    spread(3, False)

    mid_tx[...] = acc[kk:, :].astype(jnp.bfloat16)
    first = send("m1", mid_tx, mid_rx, partner)
    first.wait_recv()
    total = acc[:kk, :] + mid_rx[...].astype(jnp.float32)
    loads[4].wait()
    gain = gains[...].astype(jnp.float32)
    sr, gr = total[:per, :width] * spec_scale, total[:per, width:] * wave_scale
    si, gi = total[per:, :width] * spec_scale, total[per:, width:] * wave_scale
    gfilt_ref[...] = gr * sr + gi * si
    ebuf[:per, :width] = (gain * gr * spec_scale).astype(jnp.bfloat16)
    ebuf[:per, width:] = (gain * sr * wave_scale).astype(jnp.bfloat16)
    ebuf[per:kk, :width] = (gain * gi * spec_scale).astype(jnp.bfloat16)
    ebuf[per:kk, width:] = (gain * si * wave_scale).astype(jnp.bfloat16)
    second = send("m2", ebuf.at[:kk], ebuf.at[kk:], partner)
    second.wait_recv()
    dt[...] = jnp.transpose(ebuf[:, :width].astype(jnp.float32)).astype(jnp.bfloat16)

    tall = pf.shape[2]
    cols = 2 * own
    halves = block // cols

    def fold(r):
        def one(h, _):
            at = pl.ds(pl.multiple_of(h * cols, cols), cols)
            trig = cs[r, :, at]
            grad = jnp.dot(dt[...], trig, preferred_element_type=jnp.float32)
            ab = lax.dot_general(
                ebuf[...], joined[r, at, :], (((1,), (1,)), ((), ())),
                preferred_element_type=jnp.float32,
            )
            sums = [jnp.zeros((1, cols), jnp.float32)] * 3
            for g in range(2):
                lo = g * kk
                dth = (
                    trig[lo : lo + per].astype(jnp.float32) * ab[lo + per : lo + kk]
                    - trig[lo + per : lo + kk].astype(jnp.float32) * ab[lo : lo + per]
                )
                for d in range(3):
                    k = jnp.concatenate([kcol[d, g * per : (g + 1) * per, :]] * (cols // LANES), 1)
                    sums[d] = sums[d] + jnp.sum(dth * k, axis=0, keepdims=True)
            rest = jnp.zeros((tall - width - 3, cols), jnp.float32)
            tail = jnp.concatenate(sums + [rest], 0)
            for j in range(2):
                lane = slice(j * own, (j + 1) * own)
                pf[r, h * 2 + j, :width, :] = grad[:, lane]
                pf[r, h * 2 + j, width:, :] = tail[:, lane]
            return 0

        lax.fori_loop(0, halves, one, 0)

    def give(r, q, to, dst, *extra):
        value = pf[r, zq[q]]
        for e in extra:
            value = value + e[...].astype(jnp.float32)
        sb[r, q] = value.astype(jnp.bfloat16)
        got["g", r, q] = send(("g", r, q), sb.at[r, q], dst, to)

    fold(3)
    for q in reversed(range(nz)):
        give(3, q, near[1] if q < half else near[2], rx.at[2, q])
    fold(1)
    fold(2)
    for q in reversed(range(nz)):
        if q >= half:
            give(2, q, near[2], rx.at[1, q])
            got["g", 3, q].wait_recv()
            give(1, q, near[1], rx.at[0, q], rx.at[2, q])
        else:
            give(1, q, near[1], rx.at[0, q])
            got["g", 3, q].wait_recv()
            give(2, q, near[2], rx.at[1, q], rx.at[2, q])
    fold(0)
    for q in reversed(range(1, nz)):
        got["g", 1, q].wait_recv()
        got["g", 2, q].wait_recv()
        give(0, q, far[q], rz.at[q], rx.at[0, q], rx.at[1, q])
    got["g", 1, 0].wait_recv()
    got["g", 2, 0].wait_recv()
    out = pf[0, zq[0]] + rx[0, 0].astype(jnp.float32) + rx[1, 0].astype(jnp.float32)
    for q in reversed(range(1, nz)):
        got["g", 0, q].wait_recv()
        out = out + rz[q].astype(jnp.float32)
    gfeat_ref[...] = jnp.transpose(out[:width]).astype(jnp.bfloat16)
    gpos_ref[...] = out[width : width + 3]
    for c in pending:
        c.wait_send()


def fused(nz, beads_all, positions, features, cotangent, wavevectors, filter_gain):
    own, width = features.shape
    per = filter_gain.shape[0]
    block = nz * own
    tall = width + 16
    copies = 3 + PLANE * nz + 3 + PLANE * nz
    spec_scale = 1.0 / math.sqrt(beads_all)
    wave_scale = 1.0 / math.sqrt(wavevectors.shape[1])
    bf, f32 = jnp.bfloat16, jnp.float32
    vmem = pl.BlockSpec(memory_space=pltpu.VMEM)
    return pl.pallas_call(
        functools.partial(kernel, nz, spec_scale, wave_scale),
        out_shape=(
            jax.ShapeDtypeStruct((own, width), bf),
            jax.ShapeDtypeStruct((3, own), f32),
            jax.ShapeDtypeStruct((per, width), f32),
        ),
        in_specs=[pl.BlockSpec(memory_space=pltpu.HBM)] * 5,
        out_specs=(vmem,) * 3,
        scratch_shapes=[
            pltpu.VMEM((PLANE, 3, block), f32),
            pltpu.VMEM((PLANE, block, 2 * width), bf),
            pltpu.VMEM((3, 2 * per, LANES), f32),
            pltpu.VMEM((PLANE, 4 * per, block), bf),
            pltpu.VMEM((4 * per, 2 * width), f32),
            pltpu.VMEM((2 * per, 2 * width), bf),
            pltpu.VMEM((2 * per, 2 * width), bf),
            pltpu.VMEM((4 * per, 2 * width), bf),
            pltpu.VMEM((width, 4 * per), bf),
            pltpu.VMEM((PLANE, nz, tall, own), f32),
            pltpu.VMEM((PLANE, nz, tall, own), bf),
            pltpu.VMEM((3, nz, tall, own), bf),
            pltpu.VMEM((nz, tall, own), bf),
            pltpu.SemaphoreType.DMA((copies,)),
            pltpu.SemaphoreType.DMA((copies,)),
            pltpu.SemaphoreType.DMA((5,)),
            pltpu.VMEM(wavevectors.shape, f32),
            pltpu.VMEM((per, width), bf),
        ],
        compiler_params=pltpu.CompilerParams(
            collective_id=0, has_side_effects=True, vmem_limit_bytes=40 << 20
        ),
    )(positions, features, cotangent, wavevectors, filter_gain)


def phases(pos, kvec):
    return (
        pos[0][:, None] * kvec[0][None, :]
        + pos[1][:, None] * kvec[1][None, :]
        + pos[2][:, None] * kvec[2][None, :]
    )


def contract_rows(left, right):
    return lax.dot_general(
        left, right, (((1,), (1,)), ((), ())), preferred_element_type=jnp.float32
    )


def contract_cols(left, right):
    return lax.dot_general(
        left, right, (((0,), (0,)), ((), ())), preferred_element_type=jnp.float32
    )


def filtered_spectra(term, gains, width):
    spec_r = term[:, :width]
    spec_i = term[:, width : 2 * width]
    cot_r = term[:, 2 * width : 3 * width]
    cot_i = term[:, 3 * width :]
    grad_filter = cot_r * spec_r + cot_i * spec_i
    stacked = jnp.concatenate(
        [gains * spec_r, gains * spec_i, gains * cot_r, gains * cot_i], 1
    ).astype(jnp.bfloat16)
    return (stacked, grad_filter)


def body(positions, features, cotangent, wavevectors, filter_gain):
    n_beads = lax.axis_size("beads")
    n_waves = lax.axis_size("waves")
    feats, cots = (
        lax.all_gather(features, "waves", axis=0, tiled=True),
        lax.all_gather(cotangent, "waves", axis=0, tiled=True),
    )
    beads_dev = feats.shape[0]
    width = feats.shape[1]
    waves_all = wavevectors.shape[1]
    per_owner = waves_all // (n_beads * n_waves)
    waves_dev = per_owner * n_beads
    spec_scale = 1.0 / math.sqrt(beads_dev * n_beads)
    wave_scale = 1.0 / math.sqrt(waves_all)
    grid = wavevectors.reshape(3, n_beads, n_waves, per_owner)
    local_waves = lax.dynamic_slice_in_dim(grid, lax.axis_index("waves"), 1, 2).reshape(
        3, waves_dev
    )
    joined = jnp.concatenate([feats, cots], 1)
    block = min(512, waves_dev)
    turns = waves_dev // block

    def fold_step(carry, piece, start):
        grad_feat, grad_pos = carry
        count = piece.shape[0]
        kvec = lax.dynamic_slice_in_dim(local_waves, start, count, 1)
        theta = phases(positions, kvec)
        cosine = jnp.cos(theta).astype(jnp.bfloat16)
        sine = jnp.sin(theta).astype(jnp.bfloat16)
        filt_r = piece[:, :width]
        filt_i = piece[:, width : 2 * width]
        dspec_r = piece[:, 2 * width : 3 * width]
        dspec_i = piece[:, 3 * width :]
        feat_term = (
            jnp.dot(cosine, dspec_r, preferred_element_type=jnp.float32)
            + jnp.dot(sine, dspec_i, preferred_element_type=jnp.float32)
        ) * spec_scale
        first = (
            contract_rows(cots, filt_r) * wave_scale + contract_rows(feats, dspec_r) * spec_scale
        )
        second = (
            contract_rows(cots, filt_i) * wave_scale + contract_rows(feats, dspec_i) * spec_scale
        )
        dtheta = -sine.astype(jnp.float32) * first + cosine.astype(jnp.float32) * second
        pos_term = lax.dot_general(
            kvec,
            dtheta,
            (((1,), (1,)), ((), ())),
            precision=lax.Precision.HIGHEST,
            preferred_element_type=jnp.float32,
        )
        return (grad_feat + feat_term, grad_pos + pos_term)

    kvec = local_waves
    theta = phases(positions, kvec)
    cosine = jnp.cos(theta).astype(jnp.bfloat16)
    sine = jnp.sin(theta).astype(jnp.bfloat16)
    part_cos = contract_cols(cosine, joined)
    part_sin = contract_cols(sine, joined)
    term = lax.psum_scatter(
        jnp.concatenate(
            [
                part_cos[:, :width] * spec_scale,
                part_sin[:, :width] * spec_scale,
                part_cos[:, width:] * wave_scale,
                part_sin[:, width:] * wave_scale,
            ],
            1,
        ),
        "beads",
        scatter_dimension=0,
        tiled=True,
    )
    owned, grad_filter = filtered_spectra(term, filter_gain.astype(jnp.float32), width)
    stacked = lax.all_gather(owned, "beads", axis=0, tiled=True)

    def sweep(step, carry):
        piece = lax.dynamic_slice_in_dim(stacked, step * block, block, 0)
        return fold_step(carry, piece, step * block)

    initial = (jnp.zeros((beads_dev, width), jnp.float32), jnp.zeros((3, beads_dev), jnp.float32))
    grads = lax.fori_loop(0, turns, sweep, initial)
    grad_feat, grad_pos = (
        lax.psum_scatter(
            grads[0].astype(jnp.bfloat16), "waves", scatter_dimension=0, tiled=True
        ).astype(jnp.float32),
        lax.psum_scatter(
            grads[1].astype(jnp.bfloat16), "waves", scatter_dimension=1, tiled=True
        ).astype(jnp.float32),
    )
    return (grad_feat.astype(jnp.bfloat16), grad_pos, grad_filter)


def suits(mesh):
    return mesh.shape["beads"] == 2 * PLANE and mesh.shape["waves"] == PLANE


def solution(mesh):
    placed = (
        P(None, "beads"),
        P(("beads", "waves"), None),
        P(("beads", "waves"), None),
        P(),
        P(("beads", "waves"), None),
    )

    def run(positions, features, *rest):
        part = body
        if suits(mesh):
            part = functools.partial(fused, mesh.shape["waves"], features.shape[0])
        return jax.shard_map(
            part,
            mesh=mesh,
            in_specs=placed,
            out_specs=(
                P(("beads", "waves"), None),
                P(None, ("beads", "waves")),
                P(("beads", "waves"), None),
            ),
            check_vma=False,
        )(positions, features, *rest)

    return run
```

```python
import functools
import math

import jax
import jax.numpy as jnp
from jax import lax
from jax.experimental import pallas as pl
from jax.experimental.pallas import tpu as pltpu
from jax.sharding import PartitionSpec as P

MESH = pl.DeviceIdType.MESH
PLANE = 4
LANES = 128


def flip(i, q):
    out = i
    if q % 2:
        out = out + 1 - 2 * (i % 2)
    if q // 2:
        out = out + 2 - 4 * ((i // 2) % 2)
    return out


def sincos(theta):
    n = jnp.round(theta * (2.0 / math.pi))
    k = n.astype(jnp.int32)
    r = (theta - n * 1.5703125) - n * 4.83826794896619e-4
    r2 = r * r
    s = r + r * r2 * (-1.6666654611e-1 + r2 * (8.3321608736e-3 - r2 * 1.9515295891e-4))
    c = (1.0 - 0.5 * r2) + r2 * r2 * (
        4.166664568298827e-2 + r2 * (-1.388731625493765e-3 + r2 * 2.443315711809948e-5)
    )
    swap = (k & 1) == 1
    sv = jnp.where(swap, c, s)
    cv = jnp.where(swap, s, c)
    sv = jnp.where((k & 2) == 2, -sv, sv)
    cv = jnp.where(((k + 1) & 2) == 2, -cv, cv)
    return cv, sv


def kernel(
    nz, spec_scale, wave_scale,
    pos_ref, feat_ref, cot_ref, kvec_ref, gain_ref,
    gfeat_ref, gpos_ref, gfilt_ref,
    pos_all, joined, kcol, cs, acc, mid_tx, mid_rx, ebuf, dt, pf, sb, rx, rz,
    send_sem, recv_sem, local_sem, kvecs, gains,
):
    own = feat_ref.shape[0]
    width = feat_ref.shape[1]
    per = gain_ref.shape[0]
    block = nz * own
    kk = 2 * per
    b = lax.axis_index("beads")
    z = lax.axis_index("waves")
    core = b % 2
    plane = b // 2
    partner = (b + 1 - 2 * core, z)
    near = [None] + [(flip(plane, r) * 2 + core, z) for r in range(1, PLANE)]
    far = [None] + [(b, flip(z, q)) for q in range(1, nz)]
    zq = [flip(z, q) for q in range(nz)]
    peers = [partner] + near[1:] + far[1:]

    barrier = pltpu.get_barrier_semaphore()
    for peer in peers:
        pl.semaphore_signal(barrier, inc=1, device_id=peer, device_id_type=MESH)

    ids = {}
    pending = []

    def copy(name, src, dst, to):
        i = ids.setdefault(name, len(ids))
        return pltpu.make_async_remote_copy(
            src_ref=src, dst_ref=dst, send_sem=send_sem.at[i], recv_sem=recv_sem.at[i],
            device_id=to, device_id_type=MESH,
        )

    def send(name, src, dst, to):
        c = copy(name, src, dst, to)
        c.start()
        pending.append(c)
        return c

    def rows(q):
        return pl.ds(pl.multiple_of(zq[q] * own, own), own)

    def part(q, j):
        return pl.ds(pl.multiple_of(zq[q] * own + j * (own // 2), own // 2), own // 2)

    loads = [
        pltpu.make_async_copy(src, dst, local_sem.at[i])
        for i, (src, dst) in enumerate(
            [
                (pos_ref, pos_all.at[0]),
                (feat_ref, joined.at[0, rows(0), :width]),
                (cot_ref, joined.at[0, rows(0), width:]),
                (kvec_ref, kvecs),
                (gain_ref, gains),
            ]
        )
    ]
    for c in loads:
        c.start()
    pl.semaphore_wait(barrier, len(peers))
    for c in loads[:3]:
        c.wait()

    got = {}
    for r in range(1, PLANE):
        got["p", r] = send(("p", r), pos_all.at[0], pos_all.at[r], near[r])

    def hop(r, q, src, to):
        got[r, q] = send((r, q), joined.at[src, rows(q)], joined.at[r, rows(q)], to)

    hop(1, 0, 0, near[1])
    hop(2, 0, 0, near[2])
    got[0, 1] = send((0, 1), joined.at[0, rows(0)], joined.at[0, rows(0)], far[1])

    loads[3].wait()
    eye = lax.broadcasted_iota(jnp.int32, (per, per), 0) == lax.broadcasted_iota(
        jnp.int32, (per, per), 1
    )
    for g in range(2):
        owner = (b + g * (1 - 2 * core)) * nz + z
        piece = kvecs[:, pl.ds(pl.multiple_of(owner * per, per), per)]
        for d in range(3):
            line = jnp.where(eye, jnp.broadcast_to(piece[d : d + 1], (per, per)), 0.0)
            kcol[d, g * per : (g + 1) * per, :] = jnp.broadcast_to(
                jnp.sum(line, axis=1, keepdims=True), (per, LANES)
            )

    step = 16
    per_group = per // step
    wide = block // LANES

    def waves(r):
        p = pos_all[r]

        def one(i, _):
            at = pl.ds(pl.multiple_of(i * step, step), step)
            k0, k1, k2 = (jnp.concatenate([kcol[d, at, :]] * wide, 1) for d in range(3))
            theta = p[0:1] * k0 + p[1:2] * k1 + p[2:3] * k2
            cv, sv = sincos(theta)
            base = (i // per_group) * kk + (i % per_group) * step
            cs[r, pl.ds(pl.multiple_of(base, step), step), :] = cv.astype(jnp.bfloat16)
            cs[r, pl.ds(pl.multiple_of(base + per, step), step), :] = sv.astype(jnp.bfloat16)
            return 0

        lax.fori_loop(0, 2 * per_group, one, 0)

    def spread(r, first):
        term = jnp.dot(cs[r], joined[r], preferred_element_type=jnp.float32)
        if first:
            acc[...] = term
        else:
            acc[...] += term

    def arrive(r, q):
        got[r, q].wait_recv()

    half = nz // 2

    def post(q):
        got[0, q] = send((0, q), joined.at[0, rows(0)], joined.at[0, rows(0)], far[q])

    post(2)
    post(3)
    waves(0)
    arrive(2, 0)
    hop(3, 0, 2, near[1])
    arrive(0, 1)
    hop(1, 1, 0, near[1])
    hop(2, 1, 0, near[2])
    got["p", 1].wait_recv()
    waves(1)
    arrive(0, 2)
    hop(1, 2, 0, near[1])
    hop(2, 2, 0, near[2])
    arrive(3, 0)
    got[3, 1] = send((3, 1), joined.at[3, rows(0)], joined.at[3, rows(0)], far[1])
    got["p", 2].wait_recv()
    waves(2)
    arrive(0, 3)
    hop(1, 3, 0, near[1])
    hop(2, 3, 0, near[2])
    spread(0, True)
    arrive(1, 2)
    hop(3, 2, 1, near[2])
    got["p", 3].wait_recv()
    waves(3)
    arrive(1, 3)
    got[3, 3] = send((3, 3), joined.at[1, part(3, 0)], joined.at[3, part(3, 0)], near[2])
    arrive(2, 3)
    got[3, 4] = send((3, 4), joined.at[2, part(3, 1)], joined.at[3, part(3, 1)], near[1])
    arrive(1, 0)
    arrive(1, 1)
    spread(1, False)
    arrive(2, 1)
    arrive(2, 2)
    spread(2, False)
    for q in range(1, 5):
        arrive(3, q)
    spread(3, False)

    mid_tx[...] = acc[kk:, :].astype(jnp.bfloat16)
    first = send("m1", mid_tx, mid_rx, partner)
    first.wait_recv()
    total = acc[:kk, :] + mid_rx[...].astype(jnp.float32)
    loads[4].wait()
    gain = gains[...].astype(jnp.float32)
    sr, gr = total[:per, :width] * spec_scale, total[:per, width:] * wave_scale
    si, gi = total[per:, :width] * spec_scale, total[per:, width:] * wave_scale
    gfilt_ref[...] = gr * sr + gi * si
    ebuf[:per, :width] = (gain * gr * spec_scale).astype(jnp.bfloat16)
    ebuf[:per, width:] = (gain * sr * wave_scale).astype(jnp.bfloat16)
    ebuf[per:kk, :width] = (gain * gi * spec_scale).astype(jnp.bfloat16)
    ebuf[per:kk, width:] = (gain * si * wave_scale).astype(jnp.bfloat16)
    second = send("m2", ebuf.at[:kk], ebuf.at[kk:], partner)
    second.wait_recv()
    dt[...] = jnp.transpose(ebuf[:, :width].astype(jnp.float32)).astype(jnp.bfloat16)

    tall = pf.shape[2]
    cols = 2 * own
    halves = block // cols

    def fold(r):
        def one(h, _):
            at = pl.ds(pl.multiple_of(h * cols, cols), cols)
            trig = cs[r, :, at]
            grad = jnp.dot(dt[...], trig, preferred_element_type=jnp.float32)
            ab = lax.dot_general(
                ebuf[...], joined[r, at, :], (((1,), (1,)), ((), ())),
                preferred_element_type=jnp.float32,
            )
            sums = [jnp.zeros((1, cols), jnp.float32)] * 3
            for g in range(2):
                lo = g * kk
                dth = (
                    trig[lo : lo + per].astype(jnp.float32) * ab[lo + per : lo + kk]
                    - trig[lo + per : lo + kk].astype(jnp.float32) * ab[lo : lo + per]
                )
                for d in range(3):
                    k = jnp.concatenate([kcol[d, g * per : (g + 1) * per, :]] * (cols // LANES), 1)
                    sums[d] = sums[d] + jnp.sum(dth * k, axis=0, keepdims=True)
            rest = jnp.zeros((tall - width - 3, cols), jnp.float32)
            tail = jnp.concatenate(sums + [rest], 0)
            for j in range(2):
                lane = slice(j * own, (j + 1) * own)
                pf[r, h * 2 + j, :width, :] = grad[:, lane]
                pf[r, h * 2 + j, width:, :] = tail[:, lane]
            return 0

        lax.fori_loop(0, halves, one, 0)

    def give(r, q, to, dst, *extra):
        value = pf[r, zq[q]]
        for e in extra:
            value = value + e[...].astype(jnp.float32)
        sb[r, q] = value.astype(jnp.bfloat16)
        got["g", r, q] = send(("g", r, q), sb.at[r, q], dst, to)

    fold(3)
    for q in reversed(range(nz)):
        give(3, q, near[1] if q < half else near[2], rx.at[2, q])
    fold(1)
    fold(2)
    for q in reversed(range(nz)):
        if q >= half:
            give(2, q, near[2], rx.at[1, q])
            got["g", 3, q].wait_recv()
            give(1, q, near[1], rx.at[0, q], rx.at[2, q])
        else:
            give(1, q, near[1], rx.at[0, q])
            got["g", 3, q].wait_recv()
            give(2, q, near[2], rx.at[1, q], rx.at[2, q])
    fold(0)
    for q in reversed(range(1, nz)):
        got["g", 1, q].wait_recv()
        got["g", 2, q].wait_recv()
        give(0, q, far[q], rz.at[q], rx.at[0, q], rx.at[1, q])
    got["g", 1, 0].wait_recv()
    got["g", 2, 0].wait_recv()
    out = pf[0, zq[0]] + rx[0, 0].astype(jnp.float32) + rx[1, 0].astype(jnp.float32)
    for q in reversed(range(1, nz)):
        got["g", 0, q].wait_recv()
        out = out + rz[q].astype(jnp.float32)
    gfeat_ref[...] = jnp.transpose(out[:width]).astype(jnp.bfloat16)
    gpos_ref[...] = out[width : width + 3]
    for c in pending:
        c.wait_send()


def fused(nz, beads_all, positions, features, cotangent, wavevectors, filter_gain):
    own, width = features.shape
    per = filter_gain.shape[0]
    block = nz * own
    tall = width + 16
    copies = 3 + PLANE * nz + 3 + PLANE * nz
    spec_scale = 1.0 / math.sqrt(beads_all)
    wave_scale = 1.0 / math.sqrt(wavevectors.shape[1])
    bf, f32 = jnp.bfloat16, jnp.float32
    vmem = pl.BlockSpec(memory_space=pltpu.VMEM)
    return pl.pallas_call(
        functools.partial(kernel, nz, spec_scale, wave_scale),
        out_shape=(
            jax.ShapeDtypeStruct((own, width), bf),
            jax.ShapeDtypeStruct((3, own), f32),
            jax.ShapeDtypeStruct((per, width), f32),
        ),
        in_specs=[pl.BlockSpec(memory_space=pltpu.HBM)] * 5,
        out_specs=(vmem,) * 3,
        scratch_shapes=[
            pltpu.VMEM((PLANE, 3, block), f32),
            pltpu.VMEM((PLANE, block, 2 * width), bf),
            pltpu.VMEM((3, 2 * per, LANES), f32),
            pltpu.VMEM((PLANE, 4 * per, block), bf),
            pltpu.VMEM((4 * per, 2 * width), f32),
            pltpu.VMEM((2 * per, 2 * width), bf),
            pltpu.VMEM((2 * per, 2 * width), bf),
            pltpu.VMEM((4 * per, 2 * width), bf),
            pltpu.VMEM((width, 4 * per), bf),
            pltpu.VMEM((PLANE, nz, tall, own), f32),
            pltpu.VMEM((PLANE, nz, tall, own), bf),
            pltpu.VMEM((3, nz, tall, own), bf),
            pltpu.VMEM((nz, tall, own), bf),
            pltpu.SemaphoreType.DMA((copies,)),
            pltpu.SemaphoreType.DMA((copies,)),
            pltpu.SemaphoreType.DMA((5,)),
            pltpu.VMEM(wavevectors.shape, f32),
            pltpu.VMEM((per, width), bf),
        ],
        compiler_params=pltpu.CompilerParams(
            collective_id=0, has_side_effects=True, vmem_limit_bytes=63 << 20
        ),
    )(positions, features, cotangent, wavevectors, filter_gain)


def phases(pos, kvec):
    return (
        pos[0][:, None] * kvec[0][None, :]
        + pos[1][:, None] * kvec[1][None, :]
        + pos[2][:, None] * kvec[2][None, :]
    )


def contract_rows(left, right):
    return lax.dot_general(
        left, right, (((1,), (1,)), ((), ())), preferred_element_type=jnp.float32
    )


def contract_cols(left, right):
    return lax.dot_general(
        left, right, (((0,), (0,)), ((), ())), preferred_element_type=jnp.float32
    )


def filtered_spectra(term, gains, width):
    spec_r = term[:, :width]
    spec_i = term[:, width : 2 * width]
    cot_r = term[:, 2 * width : 3 * width]
    cot_i = term[:, 3 * width :]
    grad_filter = cot_r * spec_r + cot_i * spec_i
    stacked = jnp.concatenate(
        [gains * spec_r, gains * spec_i, gains * cot_r, gains * cot_i], 1
    ).astype(jnp.bfloat16)
    return (stacked, grad_filter)


def body(positions, features, cotangent, wavevectors, filter_gain):
    n_beads = lax.axis_size("beads")
    n_waves = lax.axis_size("waves")
    feats, cots = (
        lax.all_gather(features, "waves", axis=0, tiled=True),
        lax.all_gather(cotangent, "waves", axis=0, tiled=True),
    )
    beads_dev = feats.shape[0]
    width = feats.shape[1]
    waves_all = wavevectors.shape[1]
    per_owner = waves_all // (n_beads * n_waves)
    waves_dev = per_owner * n_beads
    spec_scale = 1.0 / math.sqrt(beads_dev * n_beads)
    wave_scale = 1.0 / math.sqrt(waves_all)
    grid = wavevectors.reshape(3, n_beads, n_waves, per_owner)
    local_waves = lax.dynamic_slice_in_dim(grid, lax.axis_index("waves"), 1, 2).reshape(
        3, waves_dev
    )
    joined = jnp.concatenate([feats, cots], 1)
    block = min(512, waves_dev)
    turns = waves_dev // block

    def fold_step(carry, piece, start):
        grad_feat, grad_pos = carry
        count = piece.shape[0]
        kvec = lax.dynamic_slice_in_dim(local_waves, start, count, 1)
        theta = phases(positions, kvec)
        cosine = jnp.cos(theta).astype(jnp.bfloat16)
        sine = jnp.sin(theta).astype(jnp.bfloat16)
        filt_r = piece[:, :width]
        filt_i = piece[:, width : 2 * width]
        dspec_r = piece[:, 2 * width : 3 * width]
        dspec_i = piece[:, 3 * width :]
        feat_term = (
            jnp.dot(cosine, dspec_r, preferred_element_type=jnp.float32)
            + jnp.dot(sine, dspec_i, preferred_element_type=jnp.float32)
        ) * spec_scale
        first = (
            contract_rows(cots, filt_r) * wave_scale + contract_rows(feats, dspec_r) * spec_scale
        )
        second = (
            contract_rows(cots, filt_i) * wave_scale + contract_rows(feats, dspec_i) * spec_scale
        )
        dtheta = -sine.astype(jnp.float32) * first + cosine.astype(jnp.float32) * second
        pos_term = lax.dot_general(
            kvec,
            dtheta,
            (((1,), (1,)), ((), ())),
            precision=lax.Precision.HIGHEST,
            preferred_element_type=jnp.float32,
        )
        return (grad_feat + feat_term, grad_pos + pos_term)

    kvec = local_waves
    theta = phases(positions, kvec)
    cosine = jnp.cos(theta).astype(jnp.bfloat16)
    sine = jnp.sin(theta).astype(jnp.bfloat16)
    part_cos = contract_cols(cosine, joined)
    part_sin = contract_cols(sine, joined)
    term = lax.psum_scatter(
        jnp.concatenate(
            [
                part_cos[:, :width] * spec_scale,
                part_sin[:, :width] * spec_scale,
                part_cos[:, width:] * wave_scale,
                part_sin[:, width:] * wave_scale,
            ],
            1,
        ),
        "beads",
        scatter_dimension=0,
        tiled=True,
    )
    owned, grad_filter = filtered_spectra(term, filter_gain.astype(jnp.float32), width)
    stacked = lax.all_gather(owned, "beads", axis=0, tiled=True)

    def sweep(step, carry):
        piece = lax.dynamic_slice_in_dim(stacked, step * block, block, 0)
        return fold_step(carry, piece, step * block)

    initial = (jnp.zeros((beads_dev, width), jnp.float32), jnp.zeros((3, beads_dev), jnp.float32))
    grads = lax.fori_loop(0, turns, sweep, initial)
    grad_feat, grad_pos = (
        lax.psum_scatter(
            grads[0].astype(jnp.bfloat16), "waves", scatter_dimension=0, tiled=True
        ).astype(jnp.float32),
        lax.psum_scatter(
            grads[1].astype(jnp.bfloat16), "waves", scatter_dimension=1, tiled=True
        ).astype(jnp.float32),
    )
    return (grad_feat.astype(jnp.bfloat16), grad_pos, grad_filter)


def suits(mesh):
    return mesh.shape["beads"] == 2 * PLANE and mesh.shape["waves"] == PLANE


def solution(mesh):
    placed = (
        P(None, "beads"),
        P(("beads", "waves"), None),
        P(("beads", "waves"), None),
        P(),
        P(("beads", "waves"), None),
    )

    def run(positions, features, *rest):
        part = body
        if suits(mesh):
            part = functools.partial(fused, mesh.shape["waves"], features.shape[0])
        return jax.shard_map(
            part,
            mesh=mesh,
            in_specs=placed,
            out_specs=(
                P(("beads", "waves"), None),
                P(None, ("beads", "waves")),
                P(("beads", "waves"), None),
            ),
            check_vma=False,
        )(positions, features, *rest)

    return run
```

```python
import functools
import math

import jax
import jax.numpy as jnp
from jax import lax
from jax.experimental import pallas as pl
from jax.experimental.pallas import tpu as pltpu
from jax.sharding import PartitionSpec as P

MESH = pl.DeviceIdType.MESH
PLANE = 4
LANES = 128


def flip(i, q):
    out = i
    if q % 2:
        out = out + 1 - 2 * (i % 2)
    if q // 2:
        out = out + 2 - 4 * ((i // 2) % 2)
    return out


def sincos(theta):
    n = jnp.round(theta * (2.0 / math.pi))
    k = n.astype(jnp.int32)
    r = (theta - n * 1.5703125) - n * 4.83826794896619e-4
    r2 = r * r
    s = r + r * r2 * (-1.6666654611e-1 + r2 * (8.3321608736e-3 - r2 * 1.9515295891e-4))
    c = (1.0 - 0.5 * r2) + r2 * r2 * (
        4.166664568298827e-2 + r2 * (-1.388731625493765e-3 + r2 * 2.443315711809948e-5)
    )
    swap = (k & 1) == 1
    sv = jnp.where(swap, c, s)
    cv = jnp.where(swap, s, c)
    sv = jnp.where((k & 2) == 2, -sv, sv)
    cv = jnp.where(((k + 1) & 2) == 2, -cv, cv)
    return cv, sv


def kernel(
    nz, spec_scale, wave_scale,
    pos_ref, feat_ref, cot_ref, kvec_ref, gain_ref,
    gfeat_ref, gpos_ref, gfilt_ref,
    pos_all, joined, kcol, cs, acc, mid_tx, mid_rx, ebuf, dt, pf, sb, rx, rz,
    send_sem, recv_sem, local_sem, kvecs, gains,
):
    own = feat_ref.shape[0]
    width = feat_ref.shape[1]
    per = gain_ref.shape[0]
    block = nz * own
    kk = 2 * per
    b = lax.axis_index("beads")
    z = lax.axis_index("waves")
    core = b % 2
    plane = b // 2
    partner = (b + 1 - 2 * core, z)
    near = [None] + [(flip(plane, r) * 2 + core, z) for r in range(1, PLANE)]
    far = [None] + [(b, flip(z, q)) for q in range(1, nz)]
    zq = [flip(z, q) for q in range(nz)]
    peers = [partner] + near[1:] + far[1:]

    barrier = pltpu.get_barrier_semaphore()
    for peer in peers:
        pl.semaphore_signal(barrier, inc=1, device_id=peer, device_id_type=MESH)

    ids = {}
    pending = []

    def copy(name, src, dst, to):
        i = ids.setdefault(name, len(ids))
        return pltpu.make_async_remote_copy(
            src_ref=src, dst_ref=dst, send_sem=send_sem.at[i], recv_sem=recv_sem.at[i],
            device_id=to, device_id_type=MESH,
        )

    def send(name, src, dst, to):
        c = copy(name, src, dst, to)
        c.start()
        pending.append(c)
        return c

    def rows(q):
        return pl.ds(pl.multiple_of(zq[q] * own, own), own)

    def part(q, j):
        return pl.ds(pl.multiple_of(zq[q] * own + j * (own // 2), own // 2), own // 2)

    loads = [
        pltpu.make_async_copy(src, dst, local_sem.at[i])
        for i, (src, dst) in enumerate(
            [
                (pos_ref, pos_all.at[0]),
                (feat_ref, joined.at[0, rows(0), :width]),
                (cot_ref, joined.at[0, rows(0), width:]),
                (kvec_ref, kvecs),
                (gain_ref, gains),
            ]
        )
    ]
    for c in loads:
        c.start()
    pl.semaphore_wait(barrier, len(peers))
    for c in loads[:3]:
        c.wait()

    got = {}
    for r in range(1, PLANE):
        got["p", r] = send(("p", r), pos_all.at[0], pos_all.at[r], near[r])

    def hop(r, q, src, to):
        got[r, q] = send((r, q), joined.at[src, rows(q)], joined.at[r, rows(q)], to)

    hop(1, 0, 0, near[1])
    hop(2, 0, 0, near[2])
    got[0, 1] = send((0, 1), joined.at[0, rows(0)], joined.at[0, rows(0)], far[1])

    loads[3].wait()
    eye = lax.broadcasted_iota(jnp.int32, (per, per), 0) == lax.broadcasted_iota(
        jnp.int32, (per, per), 1
    )
    for g in range(2):
        owner = (b + g * (1 - 2 * core)) * nz + z
        piece = kvecs[:, pl.ds(pl.multiple_of(owner * per, per), per)]
        for d in range(3):
            line = jnp.where(eye, jnp.broadcast_to(piece[d : d + 1], (per, per)), 0.0)
            kcol[d, g * per : (g + 1) * per, :] = jnp.broadcast_to(
                jnp.sum(line, axis=1, keepdims=True), (per, LANES)
            )

    step = 16
    per_group = per // step
    wide = block // LANES

    def waves(r):
        p = pos_all[r]

        def one(i, _):
            at = pl.ds(pl.multiple_of(i * step, step), step)
            k0, k1, k2 = (jnp.concatenate([kcol[d, at, :]] * wide, 1) for d in range(3))
            theta = p[0:1] * k0 + p[1:2] * k1 + p[2:3] * k2
            cv, sv = sincos(theta)
            base = (i // per_group) * kk + (i % per_group) * step
            cs[r, pl.ds(pl.multiple_of(base, step), step), :] = cv.astype(jnp.bfloat16)
            cs[r, pl.ds(pl.multiple_of(base + per, step), step), :] = sv.astype(jnp.bfloat16)
            return 0

        lax.fori_loop(0, 2 * per_group, one, 0)

    def spread(r, first):
        term = jnp.dot(cs[r], joined[r], preferred_element_type=jnp.float32)
        if first:
            acc[...] = term
        else:
            acc[...] += term

    def arrive(r, q):
        got[r, q].wait_recv()

    half = nz // 2

    def post(q):
        got[0, q] = send((0, q), joined.at[0, rows(0)], joined.at[0, rows(0)], far[q])

    post(2)
    post(3)
    waves(0)
    arrive(2, 0)
    hop(3, 0, 2, near[1])
    arrive(0, 1)
    hop(1, 1, 0, near[1])
    hop(2, 1, 0, near[2])
    got["p", 1].wait_recv()
    waves(1)
    arrive(0, 2)
    hop(1, 2, 0, near[1])
    hop(2, 2, 0, near[2])
    arrive(3, 0)
    got[3, 1] = send((3, 1), joined.at[3, rows(0)], joined.at[3, rows(0)], far[1])
    got["p", 2].wait_recv()
    waves(2)
    arrive(0, 3)
    hop(1, 3, 0, near[1])
    hop(2, 3, 0, near[2])
    spread(0, True)
    arrive(1, 2)
    hop(3, 2, 1, near[2])
    got["p", 3].wait_recv()
    waves(3)
    arrive(1, 3)
    got[3, 3] = send((3, 3), joined.at[1, part(3, 0)], joined.at[3, part(3, 0)], near[2])
    arrive(2, 3)
    got[3, 4] = send((3, 4), joined.at[2, part(3, 1)], joined.at[3, part(3, 1)], near[1])
    arrive(1, 0)
    arrive(1, 1)
    spread(1, False)
    arrive(2, 1)
    arrive(2, 2)
    spread(2, False)
    for q in range(1, 5):
        arrive(3, q)
    mid_tx[...] = (
        acc[kk:, :] + jnp.dot(cs[3, kk:, :], joined[3], preferred_element_type=jnp.float32)
    ).astype(jnp.bfloat16)
    first = send("m1", mid_tx, mid_rx, partner)
    acc[:kk, :] += jnp.dot(cs[3, :kk, :], joined[3], preferred_element_type=jnp.float32)
    first.wait_recv()
    total = acc[:kk, :] + mid_rx[...].astype(jnp.float32)
    loads[4].wait()
    gain = gains[...].astype(jnp.float32)
    sr, gr = total[:per, :width] * spec_scale, total[:per, width:] * wave_scale
    si, gi = total[per:, :width] * spec_scale, total[per:, width:] * wave_scale
    gfilt_ref[...] = gr * sr + gi * si
    ebuf[:per, :width] = (gain * gr * spec_scale).astype(jnp.bfloat16)
    ebuf[:per, width:] = (gain * sr * wave_scale).astype(jnp.bfloat16)
    ebuf[per:kk, :width] = (gain * gi * spec_scale).astype(jnp.bfloat16)
    ebuf[per:kk, width:] = (gain * si * wave_scale).astype(jnp.bfloat16)
    second = send("m2", ebuf.at[:kk], ebuf.at[kk:], partner)
    dt[:, :kk] = jnp.transpose(ebuf[:kk, :width].astype(jnp.float32)).astype(jnp.bfloat16)
    second.wait_recv()
    dt[:, kk:] = jnp.transpose(ebuf[kk:, :width].astype(jnp.float32)).astype(jnp.bfloat16)

    tall = pf.shape[2]
    cols = 2 * own
    halves = block // cols

    def fold(r):
        def one(h, _):
            at = pl.ds(pl.multiple_of(h * cols, cols), cols)
            trig = cs[r, :, at]
            grad = jnp.dot(dt[...], trig, preferred_element_type=jnp.float32)
            ab = lax.dot_general(
                ebuf[...], joined[r, at, :], (((1,), (1,)), ((), ())),
                preferred_element_type=jnp.float32,
            )
            sums = [jnp.zeros((1, cols), jnp.float32)] * 3
            for g in range(2):
                lo = g * kk
                dth = (
                    trig[lo : lo + per].astype(jnp.float32) * ab[lo + per : lo + kk]
                    - trig[lo + per : lo + kk].astype(jnp.float32) * ab[lo : lo + per]
                )
                for d in range(3):
                    k = jnp.concatenate([kcol[d, g * per : (g + 1) * per, :]] * (cols // LANES), 1)
                    sums[d] = sums[d] + jnp.sum(dth * k, axis=0, keepdims=True)
            rest = jnp.zeros((tall - width - 3, cols), jnp.float32)
            tail = jnp.concatenate(sums + [rest], 0)
            for j in range(2):
                lane = slice(j * own, (j + 1) * own)
                pf[r, h * 2 + j, :width, :] = grad[:, lane]
                pf[r, h * 2 + j, width:, :] = tail[:, lane]
            return 0

        lax.fori_loop(0, halves, one, 0)

    def give(r, q, to, dst, *extra):
        value = pf[r, zq[q]]
        for e in extra:
            value = value + e[...].astype(jnp.float32)
        sb[r, q] = value.astype(jnp.bfloat16)
        got["g", r, q] = send(("g", r, q), sb.at[r, q], dst, to)

    fold(3)
    for q in reversed(range(nz)):
        give(3, q, near[1] if q < half else near[2], rx.at[2, q])
    fold(1)
    fold(2)
    for q in reversed(range(nz)):
        if q >= half:
            give(2, q, near[2], rx.at[1, q])
            got["g", 3, q].wait_recv()
            give(1, q, near[1], rx.at[0, q], rx.at[2, q])
        else:
            give(1, q, near[1], rx.at[0, q])
            got["g", 3, q].wait_recv()
            give(2, q, near[2], rx.at[1, q], rx.at[2, q])
    fold(0)
    for q in reversed(range(1, nz)):
        got["g", 1, q].wait_recv()
        got["g", 2, q].wait_recv()
        give(0, q, far[q], rz.at[q], rx.at[0, q], rx.at[1, q])
    got["g", 1, 0].wait_recv()
    got["g", 2, 0].wait_recv()
    out = pf[0, zq[0]] + rx[0, 0].astype(jnp.float32) + rx[1, 0].astype(jnp.float32)
    for q in reversed(range(1, nz)):
        got["g", 0, q].wait_recv()
        out = out + rz[q].astype(jnp.float32)
    gfeat_ref[...] = jnp.transpose(out[:width]).astype(jnp.bfloat16)
    gpos_ref[...] = out[width : width + 3]
    for c in pending:
        c.wait_send()


def fused(nz, beads_all, positions, features, cotangent, wavevectors, filter_gain):
    own, width = features.shape
    per = filter_gain.shape[0]
    block = nz * own
    tall = width + 16
    copies = 3 + PLANE * nz + 3 + PLANE * nz
    spec_scale = 1.0 / math.sqrt(beads_all)
    wave_scale = 1.0 / math.sqrt(wavevectors.shape[1])
    bf, f32 = jnp.bfloat16, jnp.float32
    vmem = pl.BlockSpec(memory_space=pltpu.VMEM)
    return pl.pallas_call(
        functools.partial(kernel, nz, spec_scale, wave_scale),
        out_shape=(
            jax.ShapeDtypeStruct((own, width), bf),
            jax.ShapeDtypeStruct((3, own), f32),
            jax.ShapeDtypeStruct((per, width), f32),
        ),
        in_specs=[pl.BlockSpec(memory_space=pltpu.HBM)] * 5,
        out_specs=(vmem,) * 3,
        scratch_shapes=[
            pltpu.VMEM((PLANE, 3, block), f32),
            pltpu.VMEM((PLANE, block, 2 * width), bf),
            pltpu.VMEM((3, 2 * per, LANES), f32),
            pltpu.VMEM((PLANE, 4 * per, block), bf),
            pltpu.VMEM((4 * per, 2 * width), f32),
            pltpu.VMEM((2 * per, 2 * width), bf),
            pltpu.VMEM((2 * per, 2 * width), bf),
            pltpu.VMEM((4 * per, 2 * width), bf),
            pltpu.VMEM((width, 4 * per), bf),
            pltpu.VMEM((PLANE, nz, tall, own), f32),
            pltpu.VMEM((PLANE, nz, tall, own), bf),
            pltpu.VMEM((3, nz, tall, own), bf),
            pltpu.VMEM((nz, tall, own), bf),
            pltpu.SemaphoreType.DMA((copies,)),
            pltpu.SemaphoreType.DMA((copies,)),
            pltpu.SemaphoreType.DMA((5,)),
            pltpu.VMEM(wavevectors.shape, f32),
            pltpu.VMEM((per, width), bf),
        ],
        compiler_params=pltpu.CompilerParams(
            collective_id=0, has_side_effects=True, vmem_limit_bytes=63 << 20
        ),
    )(positions, features, cotangent, wavevectors, filter_gain)


def phases(pos, kvec):
    return (
        pos[0][:, None] * kvec[0][None, :]
        + pos[1][:, None] * kvec[1][None, :]
        + pos[2][:, None] * kvec[2][None, :]
    )


def contract_rows(left, right):
    return lax.dot_general(
        left, right, (((1,), (1,)), ((), ())), preferred_element_type=jnp.float32
    )


def contract_cols(left, right):
    return lax.dot_general(
        left, right, (((0,), (0,)), ((), ())), preferred_element_type=jnp.float32
    )


def filtered_spectra(term, gains, width):
    spec_r = term[:, :width]
    spec_i = term[:, width : 2 * width]
    cot_r = term[:, 2 * width : 3 * width]
    cot_i = term[:, 3 * width :]
    grad_filter = cot_r * spec_r + cot_i * spec_i
    stacked = jnp.concatenate(
        [gains * spec_r, gains * spec_i, gains * cot_r, gains * cot_i], 1
    ).astype(jnp.bfloat16)
    return (stacked, grad_filter)


def body(positions, features, cotangent, wavevectors, filter_gain):
    n_beads = lax.axis_size("beads")
    n_waves = lax.axis_size("waves")
    feats, cots = (
        lax.all_gather(features, "waves", axis=0, tiled=True),
        lax.all_gather(cotangent, "waves", axis=0, tiled=True),
    )
    beads_dev = feats.shape[0]
    width = feats.shape[1]
    waves_all = wavevectors.shape[1]
    per_owner = waves_all // (n_beads * n_waves)
    waves_dev = per_owner * n_beads
    spec_scale = 1.0 / math.sqrt(beads_dev * n_beads)
    wave_scale = 1.0 / math.sqrt(waves_all)
    grid = wavevectors.reshape(3, n_beads, n_waves, per_owner)
    local_waves = lax.dynamic_slice_in_dim(grid, lax.axis_index("waves"), 1, 2).reshape(
        3, waves_dev
    )
    joined = jnp.concatenate([feats, cots], 1)
    block = min(512, waves_dev)
    turns = waves_dev // block

    def fold_step(carry, piece, start):
        grad_feat, grad_pos = carry
        count = piece.shape[0]
        kvec = lax.dynamic_slice_in_dim(local_waves, start, count, 1)
        theta = phases(positions, kvec)
        cosine = jnp.cos(theta).astype(jnp.bfloat16)
        sine = jnp.sin(theta).astype(jnp.bfloat16)
        filt_r = piece[:, :width]
        filt_i = piece[:, width : 2 * width]
        dspec_r = piece[:, 2 * width : 3 * width]
        dspec_i = piece[:, 3 * width :]
        feat_term = (
            jnp.dot(cosine, dspec_r, preferred_element_type=jnp.float32)
            + jnp.dot(sine, dspec_i, preferred_element_type=jnp.float32)
        ) * spec_scale
        first = (
            contract_rows(cots, filt_r) * wave_scale + contract_rows(feats, dspec_r) * spec_scale
        )
        second = (
            contract_rows(cots, filt_i) * wave_scale + contract_rows(feats, dspec_i) * spec_scale
        )
        dtheta = -sine.astype(jnp.float32) * first + cosine.astype(jnp.float32) * second
        pos_term = lax.dot_general(
            kvec,
            dtheta,
            (((1,), (1,)), ((), ())),
            precision=lax.Precision.HIGHEST,
            preferred_element_type=jnp.float32,
        )
        return (grad_feat + feat_term, grad_pos + pos_term)

    kvec = local_waves
    theta = phases(positions, kvec)
    cosine = jnp.cos(theta).astype(jnp.bfloat16)
    sine = jnp.sin(theta).astype(jnp.bfloat16)
    part_cos = contract_cols(cosine, joined)
    part_sin = contract_cols(sine, joined)
    term = lax.psum_scatter(
        jnp.concatenate(
            [
                part_cos[:, :width] * spec_scale,
                part_sin[:, :width] * spec_scale,
                part_cos[:, width:] * wave_scale,
                part_sin[:, width:] * wave_scale,
            ],
            1,
        ),
        "beads",
        scatter_dimension=0,
        tiled=True,
    )
    owned, grad_filter = filtered_spectra(term, filter_gain.astype(jnp.float32), width)
    stacked = lax.all_gather(owned, "beads", axis=0, tiled=True)

    def sweep(step, carry):
        piece = lax.dynamic_slice_in_dim(stacked, step * block, block, 0)
        return fold_step(carry, piece, step * block)

    initial = (jnp.zeros((beads_dev, width), jnp.float32), jnp.zeros((3, beads_dev), jnp.float32))
    grads = lax.fori_loop(0, turns, sweep, initial)
    grad_feat, grad_pos = (
        lax.psum_scatter(
            grads[0].astype(jnp.bfloat16), "waves", scatter_dimension=0, tiled=True
        ).astype(jnp.float32),
        lax.psum_scatter(
            grads[1].astype(jnp.bfloat16), "waves", scatter_dimension=1, tiled=True
        ).astype(jnp.float32),
    )
    return (grad_feat.astype(jnp.bfloat16), grad_pos, grad_filter)


def suits(mesh):
    return mesh.shape["beads"] == 2 * PLANE and mesh.shape["waves"] == PLANE


def solution(mesh):
    placed = (
        P(None, "beads"),
        P(("beads", "waves"), None),
        P(("beads", "waves"), None),
        P(),
        P(("beads", "waves"), None),
    )

    def run(positions, features, *rest):
        part = body
        if suits(mesh):
            part = functools.partial(fused, mesh.shape["waves"], features.shape[0])
        return jax.shard_map(
            part,
            mesh=mesh,
            in_specs=placed,
            out_specs=(
                P(("beads", "waves"), None),
                P(None, ("beads", "waves")),
                P(("beads", "waves"), None),
            ),
            check_vma=False,
        )(positions, features, *rest)

    return run
```
